768 devices in a mesh: ctx: 48 (over z, x), exp: 16 (over y, core).
Axes of the slice: x: 4, y: 8, z: 12, core: 2. Of those that a mesh axis runs over, the one named last changes fastest.
Arguments:
- residual_in: bfloat16 [3072, 4096], P('ctx'), may hold values from -12 to 12
- queries: bfloat16 [3072, 8192], P('ctx', 'exp'), may hold values from -40 to 40
- projected_key_value: bfloat16 [2, 3072, 512], P(None, 'ctx'), may hold values from -40 to 40
- query_gain: float32 [128], replicated, may hold values from 0.5 to 7
- key_norm_gain: float32 [128], replicated, may hold values from 0.5 to 7
- output_weight: bfloat16 [8192, 4096], P('exp'), may hold values from -0.0625 to 0.0625
- norm_gain: float32 [4096], replicated, may hold values from 0.5 to 1.5
- gate_weight: bfloat16 [768, 4096, 128], P(('exp', 'ctx')), may hold values from -0.09375 to 0.09375
- up_weight: bfloat16 [768, 4096, 128], P(('exp', 'ctx')), may hold values from -0.09375 to 0.09375
- down_weight: bfloat16 [768, 128, 4096], P(('exp', 'ctx')), may hold values from -0.21875 to 0.21875
- expert_index: int32 [3072, 8], P('ctx'), may hold values from 0 to 127, as said below
- expert_slot: int32 [3072, 8], P('ctx'), may hold values from 0 to 7, as said below
- route_weight: float32 [3072, 8], P('ctx'), may hold values from 0.2 to 1
Outputs:
- layer_out: bfloat16 [3072, 4096], P(('ctx', 'exp'))
The draws below stay inside these ranges and needn't reach their ends.
Inputs may be any that keep to these rules, and one draw needn't show every extreme that they name: `expert_index`: A token's 8 experts are different; its k-th entry lies in the k-th of 8 equal ranges of expert numbers. `expert_slot`: within each block of 64 consecutive tokens, the choices that name one expert hold slots 0, 1, 2, ... in token order; in every block some expert is named by exactly 8 tokens.
All inputs are finite; a program needn't handle non-finite values.
Results may differ from the reference program's by a relative error of at most 0.024.
The reference program's roundings to bfloat16 on the way count: a program that leaves them out, or rounds other values in their place, can miss the bound.
Values may be sent and summed in bfloat16 or wider, within the bound.
No kernel may reach another device: no remote copies, remote signals or barrier semaphores. Data moves between devices by JAX's collectives and lax.ppermute only.
A program may use at most 64 MiB of HBM per device.

```python
import math
import jax
import jax.numpy as jnp
from jax import lax

D = 4096
QUERY_HEADS = 64
KEY_VALUE_HEADS = 4
HEAD_SIZE = 128
EXPERTS = 128
TOP = 8
FF_WIN = 768
SLICES = 6
SLICE = 128
TOK_CTX = 64
CAP = 8
WINDOW_TOKENS = 3072
N_CTX = 48


def route_tables(key):
    groups = WINDOW_TOKENS // TOK_CTX
    width = EXPERTS // TOP

    def one_block(block_key, block):
        first, second = jax.random.split(block_key)
        order = jax.random.permutation(first, TOK_CTX)
        value_rows = jax.random.permutation(second, width)
        ranked = jnp.argsort(order)
        pick = jnp.where(ranked < CAP, 0, 1 + (ranked - CAP) % (width - 1))
        chosen = value_rows[pick]
        onehot = (chosen[:, None] == jnp.arange(width)[None, :]).astype(jnp.int32)
        running = jnp.cumsum(onehot, axis=0) - 1
        placed = jnp.sum(running * onehot, axis=1)
        return (block * width + chosen, placed)

    def one_group(head_group):
        return jax.vmap(lambda block: one_block(jax.random.fold_in(key, head_group * TOP + block), block))(jnp.arange(TOP))
    chosen_all, placed_all = jax.vmap(one_group)(jnp.arange(groups))
    chosen_all = jnp.transpose(chosen_all, (0, 2, 1)).reshape(WINDOW_TOKENS, TOP)
    placed_all = jnp.transpose(placed_all, (0, 2, 1)).reshape(WINDOW_TOKENS, TOP)
    return (chosen_all.astype(jnp.int32), placed_all.astype(jnp.int32))


def draw_expert_index(key, part):
    return route_tables(key)[0]


def draw_expert_slot(key, part):
    return route_tables(key)[1]


def field_scaled(key, shape, row_shape, col_shape):
    first, second, third = jax.random.split(key, 3)
    raw = jax.random.normal(first, shape, jnp.float32)
    rows = jnp.exp(jax.random.uniform(second, row_shape, jnp.float32, math.log(0.3), math.log(3.0)))
    cols = jnp.exp(jax.random.uniform(third, col_shape, jnp.float32, math.log(0.4), math.log(4.0)))
    return raw * rows * cols


def key_field(key):
    input_field = field_scaled(key, (2, WINDOW_TOKENS, KEY_VALUE_HEADS, HEAD_SIZE), (2, WINDOW_TOKENS, KEY_VALUE_HEADS, 1), (2, 1, KEY_VALUE_HEADS, HEAD_SIZE))
    key_rows = input_field[0]
    marked = (jnp.arange(WINDOW_TOKENS) % 8 == 6)[:, None, None]
    key_rows = jnp.where(marked, key_rows, key_rows)
    return jnp.clip(jnp.stack([key_rows, input_field[1]]), -40.0, 40.0)


def query_field(key):
    query_key = jax.random.fold_in(key, 7)
    input_field = field_scaled(query_key, (WINDOW_TOKENS, QUERY_HEADS, HEAD_SIZE), (WINDOW_TOKENS, QUERY_HEADS, 1), (1, QUERY_HEADS, HEAD_SIZE))
    marked = (jnp.arange(WINDOW_TOKENS) % 8 == 7)[:, None, None]
    input_field = jnp.where(marked, input_field, input_field)
    return jnp.clip(input_field, -40.0, 40.0).reshape(WINDOW_TOKENS, QUERY_HEADS * HEAD_SIZE)


def draw_queries(key, part):
    return query_field(key).astype(jnp.bfloat16)


def draw_projected_key_value(key, part):
    input_field = key_field(key)
    return input_field.reshape(2, WINDOW_TOKENS, KEY_VALUE_HEADS * HEAD_SIZE).astype(jnp.bfloat16)


def gain_values(key, low_lo, low_hi, high_lo, high_hi):
    first, second = jax.random.split(key)
    rough = jnp.arange(HEAD_SIZE) % (HEAD_SIZE // 2) < max(1, HEAD_SIZE * 12 // 128)
    low = jax.random.uniform(first, (HEAD_SIZE,), jnp.float32, low_lo, low_hi)
    high = jax.random.uniform(second, (HEAD_SIZE,), jnp.float32, high_lo, high_hi)
    return jnp.where(rough, low, high)


def draw_query_gain(key, part):
    key = jax.random.fold_in(key, 21)
    return gain_values(key, 0.6, 1.8, 0.6, 1.8)


def draw_key_norm_gain(key, part):
    key = jax.random.fold_in(key, 22)
    return gain_values(key, 0.6, 1.8, 0.6, 1.8)


def stream_field(key):
    first, second, third = jax.random.split(key, 3)
    shape = (WINDOW_TOKENS, D)
    raw = jax.random.normal(first, shape, jnp.float32)
    rows = jnp.exp(jax.random.uniform(second, (WINDOW_TOKENS, 1), jnp.float32, math.log(0.12), math.log(1.2)))
    cols = jnp.exp(jax.random.uniform(third, (1, D), jnp.float32, math.log(0.3), math.log(3.0)))
    return jnp.clip(raw * rows * cols, -12.0, 12.0)


def draw_residual_in(key, part):
    key = jax.random.fold_in(key, 31)
    return stream_field(key).astype(jnp.bfloat16)


def steps_of(key, extent, cuts, low, top_value):
    level, own = 1.0, jax.random.fold_in(key, 6)
    for position, shards_of in cuts:
        heights = jnp.exp(jax.random.uniform(jax.random.fold_in(own, position), (shards_of,), jnp.float32, low / len(cuts), top_value / len(cuts)))
        level = level * jnp.repeat(heights, extent[position] // shards_of).reshape([-1 if axis == position else 1 for axis in range(len(extent))])
    return level


def gaussian(key, dims, deviation, bound, shards=(), kind=jnp.bfloat16):
    result = deviation * jax.random.normal(key, dims, jnp.float32)
    if shards:
        result = result * steps_of(key, dims, shards, -0.22, 0.18)
    return jnp.clip(result, -bound, bound).astype(kind)


def setup_inputs(seed: int = 0) -> dict:
    streams_of = jax.random.split(jax.random.key(seed), 14)
    return {
        "residual_in": draw_residual_in(jax.random.fold_in(streams_of[13], 71), 0),
        "queries": draw_queries(jax.random.fold_in(streams_of[13], 71), 0),
        "projected_key_value": draw_projected_key_value(jax.random.fold_in(streams_of[13], 71), 0),
        "query_gain": draw_query_gain(jax.random.fold_in(streams_of[13], 71), 0),
        "key_norm_gain": draw_key_norm_gain(jax.random.fold_in(streams_of[13], 71), 0),
        "output_weight": gaussian(streams_of[5], (QUERY_HEADS * HEAD_SIZE, D), (QUERY_HEADS * HEAD_SIZE) ** -0.5, 0.0625, ((0, 16),)),
        "norm_gain": jnp.clip(1.0 + 0.1 * jax.random.normal(streams_of[6], (D,), jnp.float32), 0.5, 1.5),
        "gate_weight": gaussian(streams_of[7], (EXPERTS * SLICES, D, SLICE), D ** -0.5, 0.09375, ((0, 768),)),
        "up_weight": gaussian(streams_of[8], (EXPERTS * SLICES, D, SLICE), D ** -0.5, 0.09375, ((0, 768),)),
        "down_weight": gaussian(streams_of[9], (EXPERTS * SLICES, SLICE, D), FF_WIN ** -0.5, 0.21875, ((0, 768),)),
        "expert_index": draw_expert_index(jax.random.fold_in(streams_of[13], 71), 0),
        "expert_slot": draw_expert_slot(jax.random.fold_in(streams_of[13], 71), 0),
        "route_weight": jnp.clip(0.2 + 0.8 * jax.random.uniform(streams_of[12], (WINDOW_TOKENS, TOP), jnp.float32) ** steps_of(streams_of[12], (WINDOW_TOKENS, TOP), ((0, 48),), -0.2, 0.2), 0.2, 1.0),
    }


THETA = 1000000.0

def apply_norm(value_rows, gain):
    mean_square = lax.optimization_barrier(jnp.mean(value_rows * value_rows, axis=-1, keepdims=True))
    return value_rows * lax.rsqrt(mean_square + 1e-06) * gain

def apply_rotation(value_rows, token_positions):
    half = value_rows.shape[-1] // 2
    inverse = THETA ** (-(jnp.arange(half, dtype=jnp.float32) * 2.0 / value_rows.shape[-1]))
    angle = token_positions.astype(jnp.float32)[:, None] * inverse[None, :]
    cosine = jnp.cos(angle)[:, None, :]
    sine = jnp.sin(angle)[:, None, :]
    first = value_rows[..., :half]
    second = value_rows[..., half:]
    return jnp.concatenate([first * cosine - second * sine, second * cosine + first * sine], axis=-1)

def reference(residual_in, queries, projected_key_value, query_gain, key_norm_gain, output_weight, norm_gain, gate_weight, up_weight, down_weight, expert_index, expert_slot, route_weight):
    token_positions = jnp.arange(WINDOW_TOKENS, dtype=jnp.int32)
    query_rot = apply_rotation(apply_norm(queries.reshape(WINDOW_TOKENS, QUERY_HEADS, HEAD_SIZE).astype(jnp.float32), query_gain), token_positions).astype(jnp.bfloat16)
    rotated_keys = apply_rotation(apply_norm(projected_key_value[0].reshape(WINDOW_TOKENS, KEY_VALUE_HEADS, HEAD_SIZE).astype(jnp.float32), key_norm_gain), token_positions).astype(jnp.bfloat16)
    value_rows = projected_key_value[1].reshape(WINDOW_TOKENS, KEY_VALUE_HEADS, HEAD_SIZE)
    head_group = QUERY_HEADS // KEY_VALUE_HEADS
    scale = 1.0 / HEAD_SIZE ** 0.5
    causal = token_positions[None, :] <= token_positions[:, None]

    def one_head(head):
        query_head = query_rot[:, head]
        key_head = rotated_keys[:, head // head_group]
        value_head = value_rows[:, head // head_group]
        scores = jnp.dot(query_head, key_head.T, preferred_element_type=jnp.float32) * scale
        peak = lax.optimization_barrier(jnp.max(jnp.where(causal, scores, -jnp.inf), axis=-1, keepdims=True))
        weights = jnp.where(causal, jnp.exp(scores - peak), 0.0)
        total = lax.optimization_barrier(jnp.sum(weights, axis=-1, keepdims=True))
        return jnp.dot(weights.astype(jnp.bfloat16), value_head, preferred_element_type=jnp.float32) / total
    heads_out = lax.map(one_head, jnp.arange(QUERY_HEADS, dtype=jnp.int32))
    attended = jnp.transpose(heads_out, (1, 0, 2)).astype(jnp.bfloat16).reshape(WINDOW_TOKENS, QUERY_HEADS * HEAD_SIZE)
    stream = residual_in.astype(jnp.float32) + jnp.dot(attended, output_weight, preferred_element_type=jnp.float32)
    normed = apply_norm(stream, norm_gain).astype(jnp.bfloat16)
    block_of = (token_positions // TOK_CTX).astype(jnp.int32)
    spread_rows = jnp.broadcast_to(normed[:, None, :], (WINDOW_TOKENS, TOP, D))
    buffer = jnp.zeros((EXPERTS, N_CTX, CAP, D), jnp.bfloat16)
    buffer = buffer.at[expert_index, block_of[:, None], expert_slot].set(spread_rows)
    gate_all = gate_weight.reshape(EXPERTS, SLICES, D, SLICE)
    up_all = up_weight.reshape(EXPERTS, SLICES, D, SLICE)
    down_all = down_weight.reshape(EXPERTS, SLICES, SLICE, D)

    def expert(packed):
        rows, gate_part, up_part, down_part = packed
        flat = rows.reshape(N_CTX * CAP, D).astype(jnp.float32)
        gate = jnp.einsum('nd,sdf->snf', flat, gate_part.astype(jnp.float32))
        upper = jnp.einsum('nd,sdf->snf', flat, up_part.astype(jnp.float32))
        act = (jax.nn.silu(gate) * upper).astype(jnp.bfloat16)
        pieces = jnp.einsum('snf,sfd->snd', act.astype(jnp.float32), down_part.astype(jnp.float32)).astype(jnp.bfloat16)
        return lax.optimization_barrier(jnp.sum(pieces.astype(jnp.float32), axis=0)).reshape(N_CTX, CAP, D)
    outputs = lax.map(expert, (buffer, gate_all, up_all, down_all))
    picked = outputs[expert_index, block_of[:, None], expert_slot]
    mixture = lax.optimization_barrier(jnp.sum(route_weight[:, :, None] * picked, axis=1))
    return (stream + mixture).astype(jnp.bfloat16)
```

```python
import jax
import jax.numpy as jnp
import numpy as np
from jax import lax
from jax.sharding import Mesh
from jax.sharding import PartitionSpec as P

QUERY_HEADS = 64
KEY_VALUE_HEADS = 4
EXPERTS = 128
SLICES = 6
CAP = 8
THETA = 1000000.0
CTX = ("z", "x")
EXP = ("y", "core")


def apply_norm(value_rows, gain):
    mean_square = jnp.mean(value_rows * value_rows, axis=-1, keepdims=True)
    return value_rows * lax.rsqrt(mean_square + 1e-06) * gain


def apply_rotation(value_rows, token_positions):
    half = value_rows.shape[-1] // 2
    inverse = THETA ** (-(jnp.arange(half, dtype=jnp.float32) * 2.0 / value_rows.shape[-1]))
    angle = token_positions.astype(jnp.float32)[:, None] * inverse[None, :]
    cosine = jnp.cos(angle)[:, None, :]
    sine = jnp.sin(angle)[:, None, :]
    first = value_rows[..., :half]
    second = value_rows[..., half:]
    return jnp.concatenate(
        [first * cosine - second * sine, second * cosine + first * sine], axis=-1
    )


def sum_over_exp(partial, n_exp):
    terms = partial.astype(jnp.bfloat16).reshape(n_exp, partial.shape[0] // n_exp, -1)
    terms = lax.all_to_all(terms, EXP, split_axis=0, concat_axis=0, tiled=True)
    return jnp.sum(terms.astype(jnp.float32), axis=0)


def body(
    residual_in,
    queries,
    projected_key_value,
    query_gain,
    key_norm_gain,
    output_weight,
    norm_gain,
    gate_weight,
    up_weight,
    down_weight,
    expert_index,
    expert_slot,
    route_weight,
):
    rows = queries.shape[0]
    head_dim = query_gain.shape[0]
    local_heads = queries.shape[1] // head_dim
    n_x = lax.axis_size("x")
    n_z = lax.axis_size("z")
    n_ctx = n_x * n_z
    n_exp = lax.axis_size("y") * lax.axis_size("core")
    core = lax.axis_index("core")
    ctx_index = lax.axis_index("z") * n_x + lax.axis_index("x")
    exp_index = lax.axis_index("y") * 2 + core

    pair = [(c, c ^ 1) for c in range(n_ctx)]
    gate_other = lax.ppermute(gate_weight, CTX, pair)
    up_other = lax.ppermute(up_weight, CTX, pair)
    down_other = lax.ppermute(down_weight, CTX, pair)

    token_positions = ctx_index * rows + jnp.arange(rows, dtype=jnp.int32)
    key_value_head = exp_index * local_heads // (QUERY_HEADS // KEY_VALUE_HEADS)
    kv_block = lax.dynamic_slice_in_dim(projected_key_value, key_value_head * head_dim, head_dim, 2)
    rotated_keys = apply_rotation(
        apply_norm(kv_block[0].astype(jnp.float32)[:, None, :], key_norm_gain), token_positions
    )[:, 0, :].astype(jnp.bfloat16)
    mine = jnp.where(core == 0, rotated_keys, kv_block[1])
    mine = lax.all_gather(mine[None], "z", axis=0, tiled=True)
    mine = lax.all_gather(mine[None], "x", axis=0, tiled=True)
    mine = mine.reshape(n_ctx * rows, head_dim)
    other = lax.ppermute(mine, "core", [(0, 1), (1, 0)])
    keys = jnp.where(core == 0, mine, other)
    values = jnp.where(core == 0, other, mine)
    key_pos = (
        jnp.arange(n_z, dtype=jnp.int32)[None, :, None] * (n_x * rows)
        + jnp.arange(n_x, dtype=jnp.int32)[:, None, None] * rows
        + jnp.arange(rows, dtype=jnp.int32)[None, None, :]
    ).reshape(n_ctx * rows)

    query_rot = apply_rotation(
        apply_norm(queries.reshape(rows, local_heads, head_dim).astype(jnp.float32), query_gain),
        token_positions,
    ).astype(jnp.bfloat16)
    scale = 1.0 / head_dim**0.5
    scores = jnp.einsum("qhd,kd->hqk", query_rot, keys, preferred_element_type=jnp.float32) * scale
    visible = (key_pos[None, :] <= token_positions[:, None])[None, :, :]
    peak = jnp.max(jnp.where(visible, scores, -1e30), axis=-1)
    weights = jnp.where(visible, jnp.exp(scores - peak[..., None]), 0.0)
    total = jnp.sum(weights, axis=-1)
    accum = jnp.einsum(
        "hqk,kd->hqd", weights.astype(jnp.bfloat16), values, preferred_element_type=jnp.float32
    )
    attended = (
        jnp.transpose(accum / total[..., None], (1, 0, 2))
        .astype(jnp.bfloat16)
        .reshape(rows, local_heads * head_dim)
    )
    partial_value = jnp.dot(attended, output_weight, preferred_element_type=jnp.float32)
    share = rows // n_exp
    own_residual = lax.dynamic_slice_in_dim(residual_in, exp_index * share, share, 0)
    own_stream = own_residual.astype(jnp.float32) + sum_over_exp(partial_value, n_exp)
    own_normed = apply_norm(own_stream, norm_gain).astype(jnp.bfloat16)
    normed = lax.all_gather(own_normed, EXP, axis=0, tiled=True)

    local = EXPERTS // n_exp
    lanes = local * CAP
    local_expert = expert_index - exp_index * local
    owned = (local_expert >= 0) & (local_expert < local)
    target = jnp.where(owned, local_expert * CAP + expert_slot, -1)
    match = target[:, :, None] == jnp.arange(lanes, dtype=jnp.int32)[None, None, :]
    select = jnp.any(match, axis=1).astype(jnp.bfloat16)
    packed = lax.dot_general(
        select, normed, (((0,), (0,)), ((), ())), preferred_element_type=jnp.float32
    ).astype(jnp.bfloat16)
    combine_weights = jnp.sum(jnp.where(match, route_weight[:, :, None], 0.0), axis=1)

    pairs, half = SLICES // 2, CAP // 2
    width = packed.shape[-1]
    outgoing = jnp.broadcast_to(
        packed.reshape(local, 1, 2, half, width), (local, pairs, 2, half, width)
    ).reshape(n_ctx, half, width)
    arrived = lax.all_to_all(outgoing, CTX, split_axis=0, concat_axis=0, tiled=True)
    arrived = arrived.reshape(n_ctx * half, width)

    def hidden(gate_part, up_part):
        gate = jnp.dot(arrived, gate_part, preferred_element_type=jnp.float32)
        upper = jnp.dot(arrived, up_part, preferred_element_type=jnp.float32)
        return (jax.nn.silu(gate) * upper).astype(jnp.bfloat16)

    pieces = jnp.dot(
        hidden(gate_weight[0], up_weight[0]), down_weight[0], preferred_element_type=jnp.float32
    ) + jnp.dot(
        hidden(gate_other[0], up_other[0]), down_other[0], preferred_element_type=jnp.float32
    )
    pieces = pieces.astype(jnp.bfloat16).reshape(n_ctx, half, width)
    returned = lax.all_to_all(pieces, CTX, split_axis=0, concat_axis=0, tiled=True)
    expert_out = jnp.sum(
        returned.reshape(local, pairs, 2, half, width).astype(jnp.float32), axis=1
    ).reshape(lanes, width)
    mixture = jnp.dot(
        combine_weights,
        expert_out,
        precision=lax.Precision.HIGHEST,
        preferred_element_type=jnp.float32,
    )
    return (own_stream + sum_over_exp(mixture, n_exp)).astype(jnp.bfloat16)


def solution(mesh):
    shape = (12, 4, 8, 2)
    fine = Mesh(np.asarray(mesh.devices).reshape(shape), CTX + EXP)
    in_specs = (
        P(CTX, None),
        P(CTX, EXP),
        P(None, CTX, None),
        P(),
        P(),
        P(EXP, None),
        P(),
        P(EXP + CTX, None, None),
        P(EXP + CTX, None, None),
        P(EXP + CTX, None, None),
        P(CTX, None),
        P(CTX, None),
        P(CTX, None),
    )
    out_specs = P(CTX + EXP, None)
    return jax.shard_map(body, mesh=fine, in_specs=in_specs, out_specs=out_specs, check_vma=False)
```

```python
import jax
import jax.numpy as jnp
import numpy as np
from jax import lax
from jax.experimental import pallas as pl
from jax.experimental.pallas import tpu as pltpu
from jax.sharding import Mesh
from jax.sharding import PartitionSpec as P

QUERY_HEADS = 64
KEY_VALUE_HEADS = 4
EXPERTS = 128
SLICES = 6
CAP = 8
THETA = 1000000.0
CTX = ("z", "x")
EXP = ("y", "core")


def apply_norm(value_rows, gain):
    mean_square = jnp.mean(value_rows * value_rows, axis=-1, keepdims=True)
    return value_rows * lax.rsqrt(mean_square + 1e-06) * gain


def apply_rotation(value_rows, token_positions):
    half = value_rows.shape[-1] // 2
    inverse = THETA ** (-(jnp.arange(half, dtype=jnp.float32) * 2.0 / value_rows.shape[-1]))
    angle = token_positions.astype(jnp.float32)[:, None] * inverse[None, :]
    cosine = jnp.cos(angle)[:, None, :]
    sine = jnp.sin(angle)[:, None, :]
    first = value_rows[..., :half]
    second = value_rows[..., half:]
    return jnp.concatenate(
        [first * cosine - second * sine, second * cosine + first * sine], axis=-1
    )


def sum_over_exp(partial, core):
    n_y = lax.axis_size("y")
    terms = partial.reshape(n_y, 2, partial.shape[0] // (2 * n_y), -1)
    keep = lax.dynamic_index_in_dim(terms, core, 1, keepdims=False)
    give = lax.dynamic_index_in_dim(terms, 1 - core, 1, keepdims=False).astype(jnp.bfloat16)
    got = lax.ppermute(give, "core", [(0, 1), (1, 0)])
    both = (keep + got.astype(jnp.float32)).astype(jnp.bfloat16)
    both = lax.all_to_all(both, "y", split_axis=0, concat_axis=0, tiled=True)
    return jnp.sum(both.astype(jnp.float32), axis=0)


def expert_kernel(steps, x_ref, ga_ref, ua_ref, gb_ref, ub_ref, da_ref, db_ref, out_ref, sums):
    step = pl.program_id(0)

    @pl.when(step == 0)
    def _():
        sums[...] = jnp.zeros_like(sums)

    x = x_ref[...]
    for i, ref in enumerate((ga_ref, ua_ref, gb_ref, ub_ref)):
        sums[i] += jnp.dot(x, ref[0], preferred_element_type=jnp.float32)

    @pl.when(step == steps - 1)
    def _():
        acts = []
        for i in (0, 2):
            gate = sums[i]
            acts.append((gate / (1.0 + jnp.exp(-gate)) * sums[i + 1]).astype(jnp.bfloat16))
        columns = 1024
        for j in range(out_ref.shape[1] // columns):
            part = pl.ds(j * columns, columns)
            out_ref[:, part] = (
                jnp.dot(acts[0], da_ref[0, :, part], preferred_element_type=jnp.float32)
                + jnp.dot(acts[1], db_ref[0, :, part], preferred_element_type=jnp.float32)
            ).astype(jnp.bfloat16)


def expert_pair(rows, gate_a, up_a, gate_b, up_b, down_a, down_b):
    count, width = rows.shape
    hidden = gate_a.shape[-1]
    steps = 8
    depth = width // steps
    into = pl.BlockSpec((1, depth, hidden), lambda k: (0, k, 0))
    back = pl.BlockSpec((1, hidden, width), lambda k: (0, 0, 0))
    return pl.pallas_call(
        lambda *refs: expert_kernel(steps, *refs),
        grid=(steps,),
        in_specs=[pl.BlockSpec((count, depth), lambda k: (0, k)), into, into, into, into, back, back],
        out_specs=pl.BlockSpec((count, width), lambda k: (0, 0)),
        out_shape=jax.ShapeDtypeStruct((count, width), jnp.bfloat16),
        scratch_shapes=[pltpu.VMEM((4, count, hidden), jnp.float32)],
        compiler_params=pltpu.CompilerParams(vmem_limit_bytes=32 * 1024 * 1024),
        cost_estimate=pl.CostEstimate(
            flops=12 * count * width * hidden,
            bytes_accessed=4 * count * width + 12 * width * hidden,
            transcendentals=2 * count * hidden,
        ),
    )(rows, gate_a, up_a, gate_b, up_b, down_a, down_b)


def body(
    residual_in,
    queries,
    projected_key_value,
    query_gain,
    key_norm_gain,
    output_weight,
    norm_gain,
    gate_weight,
    up_weight,
    down_weight,
    expert_index,
    expert_slot,
    route_weight,
):
    rows = queries.shape[0]
    head_dim = query_gain.shape[0]
    local_heads = queries.shape[1] // head_dim
    n_x = lax.axis_size("x")
    n_z = lax.axis_size("z")
    n_ctx = n_x * n_z
    n_exp = lax.axis_size("y") * lax.axis_size("core")
    core = lax.axis_index("core")
    ctx_index = lax.axis_index("z") * n_x + lax.axis_index("x")
    exp_index = lax.axis_index("y") * 2 + core

    pair = [(c, c ^ 1) for c in range(n_ctx)]
    gate_other = lax.ppermute(gate_weight, CTX, pair)
    up_other = lax.ppermute(up_weight, CTX, pair)
    down_other = lax.ppermute(down_weight, CTX, pair)

    token_positions = ctx_index * rows + jnp.arange(rows, dtype=jnp.int32)
    key_value_head = exp_index * local_heads // (QUERY_HEADS // KEY_VALUE_HEADS)
    kv_block = lax.dynamic_slice_in_dim(projected_key_value, key_value_head * head_dim, head_dim, 2)
    rotated_keys = apply_rotation(
        apply_norm(kv_block[0].astype(jnp.float32)[:, None, :], key_norm_gain), token_positions
    )[:, 0, :].astype(jnp.bfloat16)
    mine = jnp.where(core == 0, rotated_keys, kv_block[1])
    mine = lax.all_gather(mine[None], "z", axis=0, tiled=True)
    mine, gate_other = lax.optimization_barrier((mine, gate_other))
    mine = lax.all_gather(mine[None], "x", axis=0, tiled=True)
    mine = mine.reshape(n_ctx * rows, head_dim)
    other = lax.ppermute(mine, "core", [(0, 1), (1, 0)])
    keys = jnp.where(core == 0, mine, other)
    values = jnp.where(core == 0, other, mine)
    key_pos = (
        jnp.arange(n_z, dtype=jnp.int32)[None, :, None] * (n_x * rows)
        + jnp.arange(n_x, dtype=jnp.int32)[:, None, None] * rows
        + jnp.arange(rows, dtype=jnp.int32)[None, None, :]
    ).reshape(n_ctx * rows)

    query_rot = apply_rotation(
        apply_norm(queries.reshape(rows, local_heads, head_dim).astype(jnp.float32), query_gain),
        token_positions,
    ).astype(jnp.bfloat16)
    scale = 1.0 / head_dim**0.5
    scores = jnp.einsum("qhd,kd->hqk", query_rot, keys, preferred_element_type=jnp.float32) * scale
    visible = (key_pos[None, :] <= token_positions[:, None])[None, :, :]
    peak = jnp.max(jnp.where(visible, scores, -1e30), axis=-1)
    weights = jnp.where(visible, jnp.exp(scores - peak[..., None]), 0.0)
    total = jnp.sum(weights, axis=-1)
    accum = jnp.einsum(
        "hqk,kd->hqd", weights.astype(jnp.bfloat16), values, preferred_element_type=jnp.float32
    )
    attended = (
        jnp.transpose(accum / total[..., None], (1, 0, 2))
        .astype(jnp.bfloat16)
        .reshape(rows, local_heads * head_dim)
    )
    partial_value = jnp.dot(attended, output_weight, preferred_element_type=jnp.float32)
    share = rows // n_exp
    own_residual = lax.dynamic_slice_in_dim(residual_in, exp_index * share, share, 0)
    own_stream = own_residual.astype(jnp.float32) + sum_over_exp(partial_value, core)
    own_stream, up_other = lax.optimization_barrier((own_stream, up_other))
    own_normed = apply_norm(own_stream, norm_gain).astype(jnp.bfloat16)
    normed = lax.all_gather(own_normed, EXP, axis=0, tiled=True)

    local = EXPERTS // n_exp
    pairs, half = SLICES // 2, CAP // 2
    lanes = n_ctx * half
    lane = jnp.arange(lanes, dtype=jnp.int32)
    lane_expert = lane // (pairs * CAP) + exp_index * local
    lane_slot = lane // half % 2 * half + lane % half
    match = (expert_index[:, :, None] == lane_expert) & (expert_slot[:, :, None] == lane_slot)
    select = jnp.any(match, axis=1).astype(jnp.bfloat16)
    combine = jnp.sum(jnp.where(match, route_weight[:, :, None], 0.0), axis=1)
    combine_high = combine.astype(jnp.bfloat16)
    combine_low = (combine - combine_high.astype(jnp.float32)).astype(jnp.bfloat16)

    outgoing = lax.dot_general(
        select, normed, (((0,), (0,)), ((), ())), preferred_element_type=jnp.float32
    ).astype(jnp.bfloat16)
    width = normed.shape[-1]
    outgoing = outgoing.reshape(n_ctx, half, width)
    arrived = lax.all_to_all(outgoing, CTX, split_axis=0, concat_axis=0, tiled=True)
    pieces = expert_pair(
        arrived.reshape(lanes, width),
        gate_weight,
        up_weight,
        gate_other,
        up_other,
        down_weight,
        down_other,
    ).reshape(n_ctx, half, width)
    returned = lax.all_to_all(pieces, CTX, split_axis=0, concat_axis=0, tiled=True)
    returned = returned.reshape(lanes, width)
    mixture = jnp.dot(combine_high, returned, preferred_element_type=jnp.float32) + jnp.dot(
        combine_low, returned, preferred_element_type=jnp.float32
    )
    return (own_stream + sum_over_exp(mixture, core)).astype(jnp.bfloat16)


def solution(mesh):
    shape = (12, 4, 8, 2)
    fine = Mesh(np.asarray(mesh.devices).reshape(shape), CTX + EXP)
    in_specs = (
        P(CTX, None),
        P(CTX, EXP),
        P(None, CTX, None),
        P(),
        P(),
        P(EXP, None),
        P(),
        P(EXP + CTX, None, None),
        P(EXP + CTX, None, None),
        P(EXP + CTX, None, None),
        P(CTX, None),
        P(CTX, None),
        P(CTX, None),
    )
    out_specs = P(CTX + EXP, None)
    return jax.shard_map(body, mesh=fine, in_specs=in_specs, out_specs=out_specs, check_vma=False)
```

```python
import jax
import jax.numpy as jnp
import numpy as np
from jax import lax
from jax.experimental import pallas as pl
from jax.experimental.pallas import tpu as pltpu
from jax.sharding import Mesh
from jax.sharding import PartitionSpec as P

QUERY_HEADS = 64
KEY_VALUE_HEADS = 4
EXPERTS = 128
SLICES = 6
CAP = 8
THETA = 1000000.0
CTX = ("z", "xh", "xl")
EXP = ("y", "core")
SWAP = [(0, 1), (1, 0)]


def tables(tokens, head_dim):
    half = head_dim // 2
    inverse = np.float32(THETA) ** (-(np.arange(half, dtype=np.float32) * 2.0 / head_dim))
    angle = np.arange(tokens, dtype=np.float32)[:, None] * inverse.astype(np.float32)[None, :]
    return np.concatenate([np.cos(angle), np.sin(angle)], axis=1).astype(np.float32)


def norm_rotate(rows, gain, table):
    half = rows.shape[-1] // 2
    mean_square = jnp.mean(rows * rows, axis=-1, keepdims=True)
    rows = rows * lax.rsqrt(mean_square + 1e-06) * gain
    first, second = rows[:, :half], rows[:, half:]
    cosine, sine = table[:, :half], table[:, half:]
    return jnp.concatenate(
        [first * cosine - second * sine, second * cosine + first * sine], axis=-1
    )


def prepare_kernel(place_ref, kv_ref, q_ref, key_gain_ref, query_gain_ref, table_ref, mine_ref, query_ref):
    rows, head_dim = mine_ref.shape
    table = table_ref[...]
    keys = norm_rotate(kv_ref[0].astype(jnp.float32), key_gain_ref[...], table)
    mine_ref[...] = jnp.where(place_ref[0] == 0, keys.astype(jnp.bfloat16), kv_ref[1])
    for h in range(q_ref.shape[1] // head_dim):
        head = q_ref[:, h * head_dim : (h + 1) * head_dim].astype(jnp.float32)
        query_ref[h * rows : (h + 1) * rows, :] = norm_rotate(
            head, query_gain_ref[...], table
        ).astype(jnp.bfloat16)


def prepare(place, key_value, queries, key_gain, query_gain, table):
    rows, width = queries.shape
    head_dim = table.shape[1]
    fixed = lambda i, place: (0, 0)
    return pl.pallas_call(
        prepare_kernel,
        grid_spec=pltpu.PrefetchScalarGridSpec(
            num_scalar_prefetch=1,
            grid=(1,),
            in_specs=[
                pl.BlockSpec((2, rows, head_dim), lambda i, place: (0, 0, place[2])),
                pl.BlockSpec((rows, width), fixed),
                pl.BlockSpec((1, head_dim), fixed),
                pl.BlockSpec((1, head_dim), fixed),
                pl.BlockSpec((rows, head_dim), lambda i, place: (place[1], 0)),
            ],
            out_specs=[
                pl.BlockSpec((rows, head_dim), fixed),
                pl.BlockSpec((rows * width // head_dim, head_dim), fixed),
            ],
        ),
        out_shape=[
            jax.ShapeDtypeStruct((rows, head_dim), jnp.bfloat16),
            jax.ShapeDtypeStruct((rows * width // head_dim, head_dim), jnp.bfloat16),
        ],
        compiler_params=pltpu.CompilerParams(vmem_limit_bytes=62 * 1024 * 1024),
    )(place, key_value, queries, key_gain, query_gain, table)


def attention_kernel(chunks, n_x, rows, place_ref, query_ref, mine_ref, other_ref, out_ref, scores):
    total_keys, head_dim = mine_ref.shape
    heads = query_ref.shape[0] // rows
    size = total_keys // chunks
    core, ctx_index = place_ref[0], place_ref[1]
    scale = 1.0 / head_dim**0.5
    query = query_ref[...]
    token = ctx_index * rows + lax.broadcasted_iota(jnp.int32, (rows, size), 0)
    key = lax.broadcasted_iota(jnp.int32, (rows, size), 1)
    key = (key // rows) * (n_x * rows) + key % rows
    peak = None
    for j in range(chunks):
        part = pl.ds(j * size, size)
        keys = jnp.where(core == 0, mine_ref[part, :], other_ref[part, :])
        found = (
            lax.dot_general(
                query, keys, (((1,), (1,)), ((), ())), preferred_element_type=jnp.float32
            )
            * scale
        )
        visible = jnp.concatenate([key + j * rows <= token] * heads, axis=0)
        found = jnp.where(visible, found, -1e30)
        scores[:, part] = found
        top = jnp.max(found, axis=-1, keepdims=True)
        peak = top if peak is None else jnp.maximum(peak, top)
    total = jnp.zeros_like(peak)
    accum = jnp.zeros((heads * rows, head_dim), jnp.float32)
    for j in range(chunks):
        part = pl.ds(j * size, size)
        values = jnp.where(core == 0, other_ref[part, :], mine_ref[part, :])
        weights = jnp.exp(scores[:, part] - peak)
        total += jnp.sum(weights, axis=-1, keepdims=True)
        accum += jnp.dot(
            weights.astype(jnp.bfloat16), values, preferred_element_type=jnp.float32
        )
    attended = (accum / total).astype(jnp.bfloat16)
    attended = jnp.concatenate(
        [attended[h * rows : (h + 1) * rows] for h in range(heads)], axis=1
    )
    place = lax.broadcasted_iota(jnp.int32, (rows, rows), 0)
    keeper = jnp.where(place < rows // 2, 1 - core, core)
    place = place % (rows // 2)
    source = (place // 4) * 8 + keeper * 4 + place % 4
    order = (source == lax.broadcasted_iota(jnp.int32, (rows, rows), 1)).astype(jnp.float32)
    out_ref[...] = jnp.dot(
        order.astype(jnp.bfloat16), attended, preferred_element_type=jnp.float32
    ).astype(jnp.bfloat16)


def attend(place, query, mine, other, rows, n_x):
    count, head_dim = query.shape
    total_keys = mine.shape[0]
    whole = pl.BlockSpec(memory_space=pltpu.VMEM)
    return pl.pallas_call(
        lambda *refs: attention_kernel(n_x, n_x, rows, *refs),
        in_specs=[pl.BlockSpec(memory_space=pltpu.SMEM)] + [whole] * 3,
        out_specs=whole,
        out_shape=jax.ShapeDtypeStruct((rows, count // rows * head_dim), jnp.bfloat16),
        scratch_shapes=[pltpu.VMEM((count, total_keys), jnp.float32)],
        compiler_params=pltpu.CompilerParams(vmem_limit_bytes=20 * 1024 * 1024),
        cost_estimate=pl.CostEstimate(
            flops=4 * count * head_dim * total_keys,
            bytes_accessed=16 * 1024 * 1024,
            transcendentals=count * total_keys,
        ),
    )(place, query, mine, other)


def expert_kernel(chunks, *refs):
    x_ref, ga_ref, ua_ref, gb_ref, ub_ref, da_ref, db_ref, out_ref, x, into, back, out, sems = refs
    width = x.shape[1]
    hidden = back.shape[0] // 2
    depth = width // chunks
    parts = [pl.ds(j * depth, depth) for j in range(chunks)]
    pairs = []
    for part in parts:
        group = [(x_ref.at[:, part], x.at[:, part])]
        for i, ref in enumerate((ga_ref, gb_ref, ua_ref, ub_ref)):
            group.append((ref.at[0, part, :], into.at[part, pl.ds(i * hidden, hidden)]))
        pairs.append(group)
    pairs.append(
        [
            (ref.at[0], back.at[pl.ds(i * hidden, hidden), :])
            for i, ref in enumerate((da_ref, db_ref))
        ]
    )
    copies = [
        [
            pltpu.make_async_copy(source, target, sems.at[j * 5 + i])
            for i, (source, target) in enumerate(group)
        ]
        for j, group in enumerate(pairs)
    ]
    for group in copies:
        for copy in group:
            copy.start()
    sums = None
    for j, part in enumerate(parts):
        for copy in copies[j]:
            copy.wait()
        term = jnp.dot(x[:, part], into[part, :], preferred_element_type=jnp.float32)
        sums = term if sums is None else sums + term
    gate, upper = sums[:, : 2 * hidden], sums[:, 2 * hidden :]
    act = (gate / (1.0 + jnp.exp(-gate)) * upper).astype(jnp.bfloat16)
    for copy in copies[chunks]:
        copy.wait()
    results = []
    for j, part in enumerate(parts):
        out[:, part] = jnp.dot(act, back[:, part], preferred_element_type=jnp.float32).astype(
            jnp.bfloat16
        )
        results.append(
            pltpu.make_async_copy(out.at[:, part], out_ref.at[:, part], sems.at[chunks * 5 + 2 + j])
        )
        results[-1].start()
    for copy in results:
        copy.wait()


def expert_pair(rows, gate_a, up_a, gate_b, up_b, down_a, down_b):
    count, width = rows.shape
    hidden = gate_a.shape[-1]
    chunks = 4
    anywhere = pl.BlockSpec(memory_space=pl.ANY)
    return pl.pallas_call(
        lambda *refs: expert_kernel(chunks, *refs),
        in_specs=[anywhere] * 7,
        out_specs=anywhere,
        out_shape=jax.ShapeDtypeStruct((count, width), jnp.bfloat16),
        scratch_shapes=[
            pltpu.VMEM((count, width), jnp.bfloat16),
            pltpu.VMEM((width, 4 * hidden), jnp.bfloat16),
            pltpu.VMEM((2 * hidden, width), jnp.bfloat16),
            pltpu.VMEM((count, width), jnp.bfloat16),
            pltpu.SemaphoreType.DMA((chunks * 6 + 2,)),
        ],
        compiler_params=pltpu.CompilerParams(vmem_limit_bytes=60 * 1024 * 1024),
        cost_estimate=pl.CostEstimate(
            flops=12 * count * width * hidden,
            bytes_accessed=4 * count * width + 12 * width * hidden,
            transcendentals=2 * count * hidden,
        ),
    )(rows, gate_a, up_a, gate_b, up_b, down_a, down_b)


def shares_over_exp(give, keep):
    n_y = lax.axis_size("y")
    got = lax.ppermute(give.astype(jnp.bfloat16), "core", SWAP)
    both = (keep + got.astype(jnp.float32)).astype(jnp.bfloat16)
    both = both.reshape(n_y, both.shape[0] // n_y, -1)
    return lax.all_to_all(both, "y", split_axis=0, concat_axis=0, tiled=True)


def add_terms(ref):
    total = ref[0].astype(jnp.float32)
    for i in range(1, ref.shape[0]):
        total += ref[i].astype(jnp.float32)
    return total


def stream_kernel(terms_ref, residual_ref, gain_ref, stream_ref, normed_ref):
    stream = residual_ref[...].astype(jnp.float32) + add_terms(terms_ref)
    mean_square = jnp.mean(stream * stream, axis=-1, keepdims=True)
    stream_ref[...] = stream
    normed_ref[...] = (stream * lax.rsqrt(mean_square + 1e-06) * gain_ref[...]).astype(
        jnp.bfloat16
    )


def finish_kernel(terms_ref, stream_ref, out_ref):
    out_ref[...] = (stream_ref[...] + add_terms(terms_ref)).astype(jnp.bfloat16)


def on_vmem(kernel, out_shape, *arguments):
    whole = pl.BlockSpec(memory_space=pltpu.VMEM)
    return pl.pallas_call(
        kernel,
        in_specs=[whole] * len(arguments),
        out_specs=jax.tree.map(lambda _: whole, out_shape),
        out_shape=out_shape,
        compiler_params=pltpu.CompilerParams(vmem_limit_bytes=4 * 1024 * 1024),
    )(*arguments)


def body(
    residual_in,
    queries,
    projected_key_value,
    query_gain,
    key_norm_gain,
    output_weight,
    norm_gain,
    gate_weight,
    up_weight,
    down_weight,
    expert_index,
    expert_slot,
    route_weight,
):
    rows = queries.shape[0]
    head_dim = query_gain.shape[0]
    local_heads = queries.shape[1] // head_dim
    n_x = lax.axis_size("xh") * lax.axis_size("xl")
    n_z = lax.axis_size("z")
    n_ctx = n_x * n_z
    n_exp = lax.axis_size("y") * lax.axis_size("core")
    core = lax.axis_index("core")
    ctx_index = lax.axis_index("z") * n_x + lax.axis_index("xh") * 2 + lax.axis_index("xl")
    exp_index = lax.axis_index("y") * 2 + core
    key_value_head = exp_index * local_heads // (QUERY_HEADS // KEY_VALUE_HEADS)
    place = jnp.stack([core, ctx_index, key_value_head]).astype(jnp.int32)
    table = jnp.asarray(tables(n_ctx * rows, head_dim))

    gate_other = lax.ppermute(gate_weight, "xl", SWAP)
    up_other = lax.ppermute(up_weight, "xl", SWAP)
    down_other = lax.ppermute(down_weight, "xl", SWAP)

    mine, query = prepare(
        place,
        projected_key_value,
        queries,
        key_norm_gain[None, :],
        query_gain[None, :],
        table,
    )
    mine = lax.all_gather(mine[None], "z", axis=0, tiled=True)
    mine, gate_other = lax.optimization_barrier((mine, gate_other))
    mine = lax.all_gather(mine[None], ("xh", "xl"), axis=0, tiled=True)
    mine = mine.reshape(n_ctx * rows, head_dim)
    other = lax.ppermute(mine, "core", SWAP)
    attended = attend(place, query, mine, other, rows, n_x)
    product = jnp.dot(attended, output_weight, preferred_element_type=jnp.float32)
    give, keep = product[: rows // 2], product[rows // 2 :]
    share = rows // n_exp
    own_residual = lax.dynamic_slice_in_dim(residual_in, exp_index * share, share, 0)
    width = own_residual.shape[-1]
    own_stream, own_normed = on_vmem(
        stream_kernel,
        [
            jax.ShapeDtypeStruct((share, width), jnp.float32),
            jax.ShapeDtypeStruct((share, width), jnp.bfloat16),
        ],
        shares_over_exp(give, keep),
        own_residual,
        norm_gain[None, :],
    )
    normed = lax.all_gather(own_normed, EXP, axis=0, tiled=True)
    normed, up_other = lax.optimization_barrier((normed, up_other))

    local = EXPERTS // n_exp
    pairs = SLICES // 2
    peers = local * pairs
    lanes = peers * CAP
    lane = jnp.arange(lanes, dtype=jnp.int32)
    lane_expert = lane // (pairs * CAP) + exp_index * local
    lane_slot = lane % CAP
    match = (expert_index[:, :, None] == lane_expert) & (expert_slot[:, :, None] == lane_slot)
    select = jnp.any(match, axis=1).astype(jnp.bfloat16)
    combine = jnp.sum(jnp.where(match, route_weight[:, :, None], 0.0), axis=1)
    combine = combine.reshape(n_exp // 2, 2, share, lanes)
    combine = jnp.concatenate(
        [lax.dynamic_index_in_dim(combine, i, 1, False) for i in (1 - core, core)], axis=0
    ).reshape(rows, lanes)
    combine_high = combine.astype(jnp.bfloat16)
    combine_low = (combine - combine_high.astype(jnp.float32)).astype(jnp.bfloat16)
    combine = jnp.concatenate([combine_high, combine_low], axis=0)

    outgoing = lax.dot_general(
        select, normed, (((0,), (0,)), ((), ())), preferred_element_type=jnp.float32
    ).astype(jnp.bfloat16)
    outgoing = outgoing.reshape(peers, CAP, width)
    arrived = lax.all_to_all(outgoing, ("z", "xh"), split_axis=0, concat_axis=0, tiled=True)
    pieces = expert_pair(
        arrived.reshape(lanes, width),
        gate_weight,
        up_weight,
        gate_other,
        up_other,
        down_weight,
        down_other,
    ).reshape(peers, CAP, width)
    returned = lax.all_to_all(pieces, ("z", "xh"), split_axis=0, concat_axis=0, tiled=True)
    returned = returned.reshape(lanes, width)
    mixture = jnp.dot(combine, returned, preferred_element_type=jnp.float32)
    mixture = mixture[:rows] + mixture[rows:]
    return on_vmem(
        finish_kernel,
        jax.ShapeDtypeStruct((share, width), jnp.bfloat16),
        shares_over_exp(mixture[: rows // 2], mixture[rows // 2 :]),
        own_stream,
    )


def solution(mesh):
    shape = (12, 2, 2, 8, 2)
    fine = Mesh(np.asarray(mesh.devices).reshape(shape), CTX + EXP)
    in_specs = (
        P(CTX, None),
        P(CTX, EXP),
        P(None, CTX, None),
        P(),
        P(),
        P(EXP, None),
        P(),
        P(EXP + CTX, None, None),
        P(EXP + CTX, None, None),
        P(EXP + CTX, None, None),
        P(CTX, None),
        P(CTX, None),
        P(CTX, None),
    )
    out_specs = P(CTX + EXP, None)
    return jax.shard_map(body, mesh=fine, in_specs=in_specs, out_specs=out_specs, check_vma=False)
```

```python
import jax
import jax.numpy as jnp
import numpy as np
from jax import lax
from jax.experimental import pallas as pl
from jax.experimental.pallas import tpu as pltpu
from jax.sharding import Mesh
from jax.sharding import PartitionSpec as P

QUERY_HEADS = 64
KEY_VALUE_HEADS = 4
EXPERTS = 128
SLICES = 6
CAP = 8
THETA = 1000000.0
CTX = ("z", "xh", "xl")
EXP = ("y", "core")
SWAP = [(0, 1), (1, 0)]


def tables(tokens, head_dim):
    half = head_dim // 2
    inverse = np.float32(THETA) ** (-(np.arange(half, dtype=np.float32) * 2.0 / head_dim))
    angle = np.arange(tokens, dtype=np.float32)[:, None] * inverse.astype(np.float32)[None, :]
    return np.concatenate([np.cos(angle), np.sin(angle)], axis=1).astype(np.float32)


def norm_rotate(rows, gain, table):
    half = rows.shape[-1] // 2
    mean_square = jnp.mean(rows * rows, axis=-1, keepdims=True)
    rows = rows * lax.rsqrt(mean_square + 1e-06) * gain
    first, second = rows[:, :half], rows[:, half:]
    cosine, sine = table[:, :half], table[:, half:]
    return jnp.concatenate(
        [first * cosine - second * sine, second * cosine + first * sine], axis=-1
    )


def prepare_kernel(place_ref, kv_ref, q_ref, key_gain_ref, query_gain_ref, table_ref, mine_ref, query_ref):
    rows, head_dim = mine_ref.shape
    table = table_ref[...]
    keys = norm_rotate(kv_ref[0].astype(jnp.float32), key_gain_ref[...], table)
    mine_ref[...] = jnp.where(place_ref[0] == 0, keys.astype(jnp.bfloat16), kv_ref[1])
    for h in range(q_ref.shape[1] // head_dim):
        head = q_ref[:, h * head_dim : (h + 1) * head_dim].astype(jnp.float32)
        query_ref[h * rows : (h + 1) * rows, :] = norm_rotate(
            head, query_gain_ref[...], table
        ).astype(jnp.bfloat16)


def prepare(place, key_value, queries, key_gain, query_gain, table):
    rows, width = queries.shape
    head_dim = table.shape[1]
    fixed = lambda i, place: (0, 0)
    return pl.pallas_call(
        prepare_kernel,
        grid_spec=pltpu.PrefetchScalarGridSpec(
            num_scalar_prefetch=1,
            grid=(1,),
            in_specs=[
                pl.BlockSpec((2, rows, head_dim), lambda i, place: (0, 0, place[2])),
                pl.BlockSpec((rows, width), fixed),
                pl.BlockSpec((1, head_dim), fixed),
                pl.BlockSpec((1, head_dim), fixed),
                pl.BlockSpec((rows, head_dim), lambda i, place: (place[1], 0)),
            ],
            out_specs=[
                pl.BlockSpec((rows, head_dim), fixed),
                pl.BlockSpec((rows * width // head_dim, head_dim), fixed),
            ],
        ),
        out_shape=[
            jax.ShapeDtypeStruct((rows, head_dim), jnp.bfloat16),
            jax.ShapeDtypeStruct((rows * width // head_dim, head_dim), jnp.bfloat16),
        ],
        compiler_params=pltpu.CompilerParams(vmem_limit_bytes=59 * 1024 * 1024),
    )(place, key_value, queries, key_gain, query_gain, table)


def attention_kernel(chunks, n_x, rows, place_ref, query_ref, mine_ref, other_ref, out_ref, scores):
    total_keys, head_dim = mine_ref.shape
    heads = query_ref.shape[0] // rows
    size = total_keys // chunks
    core, ctx_index = place_ref[0], place_ref[1]
    scale = 1.0 / head_dim**0.5
    query = query_ref[...]
    token = ctx_index * rows + lax.broadcasted_iota(jnp.int32, (rows, size), 0)
    key = lax.broadcasted_iota(jnp.int32, (rows, size), 1)
    key = (key // rows) * (n_x * rows) + key % rows
    peak = None
    for j in range(chunks):
        part = pl.ds(j * size, size)
        keys = jnp.where(core == 0, mine_ref[part, :], other_ref[part, :])
        found = (
            lax.dot_general(
                query, keys, (((1,), (1,)), ((), ())), preferred_element_type=jnp.float32
            )
            * scale
        )
        visible = jnp.concatenate([key + j * rows <= token] * heads, axis=0)
        found = jnp.where(visible, found, -1e30)
        scores[:, part] = found
        top = jnp.max(found, axis=-1, keepdims=True)
        peak = top if peak is None else jnp.maximum(peak, top)
    total = jnp.zeros_like(peak)
    accum = jnp.zeros((heads * rows, head_dim), jnp.float32)
    for j in range(chunks):
        part = pl.ds(j * size, size)
        values = jnp.where(core == 0, other_ref[part, :], mine_ref[part, :])
        weights = jnp.exp(scores[:, part] - peak)
        total += jnp.sum(weights, axis=-1, keepdims=True)
        accum += jnp.dot(
            weights.astype(jnp.bfloat16), values, preferred_element_type=jnp.float32
        )
    attended = (accum / total).astype(jnp.bfloat16)
    attended = jnp.concatenate(
        [attended[h * rows : (h + 1) * rows] for h in range(heads)], axis=1
    )
    place = lax.broadcasted_iota(jnp.int32, (rows, rows), 0)
    keeper = jnp.where(place < rows // 2, 1 - core, core)
    place = place % (rows // 2)
    source = (place // 4) * 8 + keeper * 4 + place % 4
    order = (source == lax.broadcasted_iota(jnp.int32, (rows, rows), 1)).astype(jnp.float32)
    out_ref[...] = jnp.dot(
        order.astype(jnp.bfloat16), attended, preferred_element_type=jnp.float32
    ).astype(jnp.bfloat16)


def attend(place, query, mine, other, rows, n_x):
    count, head_dim = query.shape
    total_keys = mine.shape[0]
    whole = pl.BlockSpec(memory_space=pltpu.VMEM)
    return pl.pallas_call(
        lambda *refs: attention_kernel(n_x, n_x, rows, *refs),
        in_specs=[pl.BlockSpec(memory_space=pltpu.SMEM)] + [whole] * 3,
        out_specs=whole,
        out_shape=jax.ShapeDtypeStruct((rows, count // rows * head_dim), jnp.bfloat16),
        scratch_shapes=[pltpu.VMEM((count, total_keys), jnp.float32)],
        compiler_params=pltpu.CompilerParams(vmem_limit_bytes=20 * 1024 * 1024),
        cost_estimate=pl.CostEstimate(
            flops=4 * count * head_dim * total_keys,
            bytes_accessed=16 * 1024 * 1024,
            transcendentals=count * total_keys,
        ),
    )(place, query, mine, other)


def expert_kernel(chunks, *refs):
    x_ref, ga_ref, ua_ref, gb_ref, ub_ref, da_ref, db_ref, out_ref, x, into, back, out, sems = refs
    width = x.shape[1]
    hidden = back.shape[0] // 2
    depth = width // chunks
    parts = [pl.ds(j * depth, depth) for j in range(chunks)]
    pairs = []
    for part in parts:
        group = [(x_ref.at[:, part], x.at[:, part])]
        for i, ref in enumerate((ga_ref, gb_ref, ua_ref, ub_ref)):
            group.append((ref.at[0, part, :], into.at[part, pl.ds(i * hidden, hidden)]))
        pairs.append(group)
    pairs.append(
        [
            (ref.at[0], back.at[pl.ds(i * hidden, hidden), :])
            for i, ref in enumerate((da_ref, db_ref))
        ]
    )
    copies = [
        [
            pltpu.make_async_copy(source, target, sems.at[j * 5 + i])
            for i, (source, target) in enumerate(group)
        ]
        for j, group in enumerate(pairs)
    ]
    for group in copies:
        for copy in group:
            copy.start()
    sums = None
    for j, part in enumerate(parts):
        for copy in copies[j]:
            copy.wait()
        term = jnp.dot(x[:, part], into[part, :], preferred_element_type=jnp.float32)
        sums = term if sums is None else sums + term
    gate, upper = sums[:, : 2 * hidden], sums[:, 2 * hidden :]
    act = (gate / (1.0 + jnp.exp(-gate)) * upper).astype(jnp.bfloat16)
    for copy in copies[chunks]:
        copy.wait()
    results = []
    for j, part in enumerate(parts):
        out[:, part] = jnp.dot(act, back[:, part], preferred_element_type=jnp.float32).astype(
            jnp.bfloat16
        )
        results.append(
            pltpu.make_async_copy(out.at[:, part], out_ref.at[:, part], sems.at[chunks * 5 + 2 + j])
        )
        results[-1].start()
    for copy in results:
        copy.wait()


def expert_pair(rows, gate_a, up_a, gate_b, up_b, down_a, down_b):
    count, width = rows.shape
    hidden = gate_a.shape[-1]
    chunks = 4
    anywhere = pl.BlockSpec(memory_space=pl.ANY)
    return pl.pallas_call(
        lambda *refs: expert_kernel(chunks, *refs),
        in_specs=[anywhere] * 7,
        out_specs=anywhere,
        out_shape=jax.ShapeDtypeStruct((count, width), jnp.bfloat16),
        scratch_shapes=[
            pltpu.VMEM((count, width), jnp.bfloat16),
            pltpu.VMEM((width, 4 * hidden), jnp.bfloat16),
            pltpu.VMEM((2 * hidden, width), jnp.bfloat16),
            pltpu.VMEM((count, width), jnp.bfloat16),
            pltpu.SemaphoreType.DMA((chunks * 6 + 2,)),
        ],
        compiler_params=pltpu.CompilerParams(vmem_limit_bytes=60 * 1024 * 1024),
        cost_estimate=pl.CostEstimate(
            flops=12 * count * width * hidden,
            bytes_accessed=4 * count * width + 12 * width * hidden,
            transcendentals=2 * count * hidden,
        ),
    )(rows, gate_a, up_a, gate_b, up_b, down_a, down_b)


def sum_over_cores(give, keep):
    n_y = lax.axis_size("y")
    got = lax.ppermute(give.astype(jnp.bfloat16), "core", SWAP)
    both = (keep + got.astype(jnp.float32)).astype(jnp.bfloat16)
    return both.reshape(n_y, both.shape[0] // n_y, -1)


def to_owners(blocks):
    return lax.all_to_all(blocks, "y", split_axis=0, concat_axis=0, tiled=True)


def add_terms(ref):
    total = ref[0].astype(jnp.float32)
    for i in range(1, ref.shape[0]):
        total += ref[i].astype(jnp.float32)
    return total


def stream_kernel(terms_ref, residual_ref, gain_ref, stream_ref, normed_ref):
    stream = residual_ref[...].astype(jnp.float32) + add_terms(terms_ref)
    mean_square = jnp.mean(stream * stream, axis=-1, keepdims=True)
    stream_ref[...] = stream
    normed_ref[...] = (stream * lax.rsqrt(mean_square + 1e-06) * gain_ref[...]).astype(
        jnp.bfloat16
    )


def finish_kernel(terms_ref, stream_ref, out_ref):
    out_ref[...] = (stream_ref[...] + add_terms(terms_ref)).astype(jnp.bfloat16)


def on_vmem(kernel, out_shape, *arguments):
    whole = pl.BlockSpec(memory_space=pltpu.VMEM)
    return pl.pallas_call(
        kernel,
        in_specs=[whole] * len(arguments),
        out_specs=jax.tree.map(lambda _: whole, out_shape),
        out_shape=out_shape,
        compiler_params=pltpu.CompilerParams(vmem_limit_bytes=4 * 1024 * 1024),
    )(*arguments)


def body(
    residual_in,
    queries,
    projected_key_value,
    query_gain,
    key_norm_gain,
    output_weight,
    norm_gain,
    gate_weight,
    up_weight,
    down_weight,
    expert_index,
    expert_slot,
    route_weight,
):
    rows = queries.shape[0]
    head_dim = query_gain.shape[0]
    local_heads = queries.shape[1] // head_dim
    n_x = lax.axis_size("xh") * lax.axis_size("xl")
    n_z = lax.axis_size("z")
    n_ctx = n_x * n_z
    n_exp = lax.axis_size("y") * lax.axis_size("core")
    core = lax.axis_index("core")
    ctx_index = lax.axis_index("z") * n_x + lax.axis_index("xh") * 2 + lax.axis_index("xl")
    exp_index = lax.axis_index("y") * 2 + core
    key_value_head = exp_index * local_heads // (QUERY_HEADS // KEY_VALUE_HEADS)
    place = jnp.stack([core, ctx_index, key_value_head]).astype(jnp.int32)
    table = jnp.asarray(tables(n_ctx * rows, head_dim))

    gate_other = lax.ppermute(gate_weight, "xl", SWAP)
    up_other = lax.ppermute(up_weight, "xl", SWAP)
    down_other = lax.ppermute(down_weight, "xl", SWAP)

    mine, query = prepare(
        place,
        projected_key_value,
        queries,
        key_norm_gain[None, :],
        query_gain[None, :],
        table,
    )
    mine = lax.all_gather(mine[None], "z", axis=0, tiled=True)
    mine, gate_other = lax.optimization_barrier((mine, gate_other))
    mine = lax.all_gather(mine[None], ("xh", "xl"), axis=0, tiled=True)
    mine = mine.reshape(n_ctx * rows, head_dim)
    other = lax.ppermute(mine, "core", SWAP)
    attended = attend(place, query, mine, other, rows, n_x)
    product = jnp.dot(attended, output_weight, preferred_element_type=jnp.float32)
    give, keep = product[: rows // 2], product[rows // 2 :]
    local = EXPERTS // n_exp
    pairs = SLICES // 2
    peers = local * pairs
    lanes = peers * CAP
    lane = jnp.arange(lanes, dtype=jnp.int32)
    lane_expert = lane // (pairs * CAP) + exp_index * local
    lane_slot = lane % CAP
    match = (expert_index[:, :, None] == lane_expert) & (expert_slot[:, :, None] == lane_slot)
    select = jnp.any(match, axis=1).astype(jnp.bfloat16)
    share = rows // n_exp
    own_residual = lax.dynamic_slice_in_dim(residual_in, exp_index * share, share, 0)
    both = sum_over_cores(give, keep)
    both, own_residual, select = lax.optimization_barrier((both, own_residual, select))
    width = own_residual.shape[-1]
    own_stream, own_normed = on_vmem(
        stream_kernel,
        [
            jax.ShapeDtypeStruct((share, width), jnp.float32),
            jax.ShapeDtypeStruct((share, width), jnp.bfloat16),
        ],
        to_owners(both),
        own_residual,
        norm_gain[None, :],
    )
    normed = lax.all_gather(own_normed, EXP, axis=0, tiled=True)
    normed, up_other = lax.optimization_barrier((normed, up_other))

    combine = jnp.sum(jnp.where(match, route_weight[:, :, None], 0.0), axis=1)
    combine = combine.reshape(n_exp // 2, 2, share, lanes)
    combine = jnp.concatenate(
        [lax.dynamic_index_in_dim(combine, i, 1, False) for i in (1 - core, core)], axis=0
    ).reshape(rows, lanes)
    combine_high = combine.astype(jnp.bfloat16)
    combine_low = (combine - combine_high.astype(jnp.float32)).astype(jnp.bfloat16)
    combine = jnp.concatenate([combine_high, combine_low], axis=0)

    outgoing = lax.dot_general(
        select, normed, (((0,), (0,)), ((), ())), preferred_element_type=jnp.float32
    ).astype(jnp.bfloat16)
    outgoing = outgoing.reshape(peers, CAP, width)
    arrived = lax.all_to_all(outgoing, ("z", "xh"), split_axis=0, concat_axis=0, tiled=True)
    pieces = expert_pair(
        arrived.reshape(lanes, width),
        gate_weight,
        up_weight,
        gate_other,
        up_other,
        down_weight,
        down_other,
    ).reshape(peers, CAP, width)
    returned = lax.all_to_all(pieces, ("z", "xh"), split_axis=0, concat_axis=0, tiled=True)
    returned = returned.reshape(lanes, width)
    mixture = jnp.dot(combine, returned, preferred_element_type=jnp.float32)
    mixture = mixture[:rows] + mixture[rows:]
    return on_vmem(
        finish_kernel,
        jax.ShapeDtypeStruct((share, width), jnp.bfloat16),
        to_owners(sum_over_cores(mixture[: rows // 2], mixture[rows // 2 :])),
        own_stream,
    )


def solution(mesh):
    shape = (12, 2, 2, 8, 2)
    fine = Mesh(np.asarray(mesh.devices).reshape(shape), CTX + EXP)
    in_specs = (
        P(CTX, None),
        P(CTX, EXP),
        P(None, CTX, None),
        P(),
        P(),
        P(EXP, None),
        P(),
        P(EXP + CTX, None, None),
        P(EXP + CTX, None, None),
        P(EXP + CTX, None, None),
        P(CTX, None),
        P(CTX, None),
        P(CTX, None),
    )
    out_specs = P(CTX + EXP, None)
    return jax.shard_map(body, mesh=fine, in_specs=in_specs, out_specs=out_specs, check_vma=False)
```

```python
import jax
import jax.numpy as jnp
import numpy as np
from jax import lax
from jax.experimental import pallas as pl
from jax.experimental.pallas import tpu as pltpu
from jax.sharding import Mesh
from jax.sharding import PartitionSpec as P

QUERY_HEADS = 64
KEY_VALUE_HEADS = 4
EXPERTS = 128
SLICES = 6
CAP = 8
THETA = 1000000.0
CTX = ("z", "xh", "xl")
EXP = ("y", "core")
SWAP = [(0, 1), (1, 0)]


def tables(tokens, head_dim):
    half = head_dim // 2
    inverse = np.float32(THETA) ** (-(np.arange(half, dtype=np.float32) * 2.0 / head_dim))
    angle = np.arange(tokens, dtype=np.float32)[:, None] * inverse.astype(np.float32)[None, :]
    return np.concatenate([np.cos(angle), np.sin(angle)], axis=1).astype(np.float32)


def norm_rotate(rows, gain, table):
    half = rows.shape[-1] // 2
    mean_square = jnp.mean(rows * rows, axis=-1, keepdims=True)
    rows = rows * lax.rsqrt(mean_square + 1e-06) * gain
    first, second = rows[:, :half], rows[:, half:]
    cosine, sine = table[:, :half], table[:, half:]
    return jnp.concatenate(
        [first * cosine - second * sine, second * cosine + first * sine], axis=-1
    )


def prepare_kernel(place_ref, kv_ref, q_ref, key_gain_ref, query_gain_ref, table_ref, mine_ref, query_ref):
    copies, rows, head_dim = mine_ref.shape
    table = table_ref[...]
    keys = norm_rotate(kv_ref[0].astype(jnp.float32), key_gain_ref[...], table)
    mine = jnp.where(place_ref[0] == 0, keys.astype(jnp.bfloat16), kv_ref[1])
    for i in range(copies):
        mine_ref[i] = mine
    for h in range(q_ref.shape[1] // head_dim):
        head = q_ref[:, h * head_dim : (h + 1) * head_dim].astype(jnp.float32)
        query_ref[h * rows : (h + 1) * rows, :] = norm_rotate(
            head, query_gain_ref[...], table
        ).astype(jnp.bfloat16)


def prepare(place, key_value, queries, key_gain, query_gain, table, copies):
    rows, width = queries.shape
    head_dim = table.shape[1]
    fixed = lambda i, place: (0, 0)
    return pl.pallas_call(
        prepare_kernel,
        grid_spec=pltpu.PrefetchScalarGridSpec(
            num_scalar_prefetch=1,
            grid=(1,),
            in_specs=[
                pl.BlockSpec((2, rows, head_dim), lambda i, place: (0, 0, place[2])),
                pl.BlockSpec((rows, width), fixed),
                pl.BlockSpec((1, head_dim), fixed),
                pl.BlockSpec((1, head_dim), fixed),
                pl.BlockSpec((rows, head_dim), lambda i, place: (place[1], 0)),
            ],
            out_specs=[
                pl.BlockSpec((copies, rows, head_dim), lambda i, place: (0, 0, 0)),
                pl.BlockSpec((rows * width // head_dim, head_dim), fixed),
            ],
        ),
        out_shape=[
            jax.ShapeDtypeStruct((copies, rows, head_dim), jnp.bfloat16),
            jax.ShapeDtypeStruct((rows * width // head_dim, head_dim), jnp.bfloat16),
        ],
        compiler_params=pltpu.CompilerParams(vmem_limit_bytes=59 * 1024 * 1024),
    )(place, key_value, queries, key_gain, query_gain, table)


def attention_kernel(chunks, n_x, rows, place_ref, query_ref, mine_ref, other_ref, out_ref, scores):
    total_keys, head_dim = mine_ref.shape
    heads = query_ref.shape[0] // rows
    size = total_keys // chunks
    core, ctx_index = place_ref[0], place_ref[1]
    scale = 1.0 / head_dim**0.5
    query = query_ref[...]
    token = ctx_index * rows + lax.broadcasted_iota(jnp.int32, (rows, size), 0)
    key = lax.broadcasted_iota(jnp.int32, (rows, size), 1)
    key = (key // rows) * (n_x * rows) + key % rows
    peak = None
    for j in range(chunks):
        part = pl.ds(j * size, size)
        keys = jnp.where(core == 0, mine_ref[part, :], other_ref[part, :])
        found = (
            lax.dot_general(
                query, keys, (((1,), (1,)), ((), ())), preferred_element_type=jnp.float32
            )
            * scale
        )
        visible = jnp.concatenate([key + j * rows <= token] * heads, axis=0)
        found = jnp.where(visible, found, -1e30)
        scores[:, part] = found
        top = jnp.max(found, axis=-1, keepdims=True)
        peak = top if peak is None else jnp.maximum(peak, top)
    total = jnp.zeros_like(peak)
    accum = jnp.zeros((heads * rows, head_dim), jnp.float32)
    for j in range(chunks):
        part = pl.ds(j * size, size)
        values = jnp.where(core == 0, other_ref[part, :], mine_ref[part, :])
        weights = jnp.exp(scores[:, part] - peak)
        total += jnp.sum(weights, axis=-1, keepdims=True)
        accum += jnp.dot(
            weights.astype(jnp.bfloat16), values, preferred_element_type=jnp.float32
        )
    attended = (accum / total).astype(jnp.bfloat16)
    attended = jnp.concatenate(
        [attended[h * rows : (h + 1) * rows] for h in range(heads)], axis=1
    )
    place = lax.broadcasted_iota(jnp.int32, (rows, rows), 0)
    keeper = jnp.where(place < rows // 2, 1 - core, core)
    place = place % (rows // 2)
    source = (place // 4) * 8 + keeper * 4 + place % 4
    order = (source == lax.broadcasted_iota(jnp.int32, (rows, rows), 1)).astype(jnp.float32)
    out_ref[...] = jnp.dot(
        order.astype(jnp.bfloat16), attended, preferred_element_type=jnp.float32
    ).astype(jnp.bfloat16)


def attend(place, query, mine, other, rows, n_x):
    count, head_dim = query.shape
    total_keys = mine.shape[0]
    whole = pl.BlockSpec(memory_space=pltpu.VMEM)
    return pl.pallas_call(
        lambda *refs: attention_kernel(n_x, n_x, rows, *refs),
        in_specs=[pl.BlockSpec(memory_space=pltpu.SMEM)] + [whole] * 3,
        out_specs=whole,
        out_shape=jax.ShapeDtypeStruct((rows, count // rows * head_dim), jnp.bfloat16),
        scratch_shapes=[pltpu.VMEM((count, total_keys), jnp.float32)],
        compiler_params=pltpu.CompilerParams(vmem_limit_bytes=20 * 1024 * 1024),
        cost_estimate=pl.CostEstimate(
            flops=4 * count * head_dim * total_keys,
            bytes_accessed=16 * 1024 * 1024,
            transcendentals=count * total_keys,
        ),
    )(place, query, mine, other)


def project_kernel(attended_ref, weight_ref, give_ref, keep_ref):
    attended = attended_ref[...]
    half = attended.shape[0] // 2
    columns = 1024
    for j in range(weight_ref.shape[1] // columns):
        part = pl.ds(j * columns, columns)
        product = jnp.dot(attended, weight_ref[:, part], preferred_element_type=jnp.float32)
        give_ref[:, part] = product[:half].astype(jnp.bfloat16)
        keep_ref[:, part] = product[half:]


def project(attended, weight):
    shape = (attended.shape[0] // 2, weight.shape[1])
    whole = pl.BlockSpec(memory_space=pltpu.VMEM)
    return pl.pallas_call(
        project_kernel,
        in_specs=[whole] * 2,
        out_specs=[whole] * 2,
        out_shape=[
            jax.ShapeDtypeStruct(shape, jnp.bfloat16),
            jax.ShapeDtypeStruct(shape, jnp.float32),
        ],
        compiler_params=pltpu.CompilerParams(vmem_limit_bytes=12 * 1024 * 1024),
        cost_estimate=pl.CostEstimate(
            flops=2 * attended.shape[0] * weight.shape[0] * weight.shape[1],
            bytes_accessed=2 * weight.shape[0] * weight.shape[1],
            transcendentals=0,
        ),
    )(attended, weight)


def expert_kernel(chunks, *refs):
    x_ref, ga_ref, ua_ref, gb_ref, ub_ref, da_ref, db_ref, out_ref, x, into, back, out, sems = refs
    width = x.shape[1]
    hidden = back.shape[0] // 2
    depth = width // chunks
    parts = [pl.ds(j * depth, depth) for j in range(chunks)]
    pairs = []
    for part in parts:
        group = [(x_ref.at[:, part], x.at[:, part])]
        for i, ref in enumerate((ga_ref, gb_ref, ua_ref, ub_ref)):
            group.append((ref.at[0, part, :], into.at[part, pl.ds(i * hidden, hidden)]))
        pairs.append(group)
    pairs.append(
        [
            (ref.at[0], back.at[pl.ds(i * hidden, hidden), :])
            for i, ref in enumerate((da_ref, db_ref))
        ]
    )
    copies = [
        [
            pltpu.make_async_copy(source, target, sems.at[j * 5 + i])
            for i, (source, target) in enumerate(group)
        ]
        for j, group in enumerate(pairs)
    ]
    for group in copies:
        for copy in group:
            copy.start()
    sums = None
    for j, part in enumerate(parts):
        for copy in copies[j]:
            copy.wait()
        term = jnp.dot(x[:, part], into[part, :], preferred_element_type=jnp.float32)
        sums = term if sums is None else sums + term
    gate, upper = sums[:, : 2 * hidden], sums[:, 2 * hidden :]
    act = (gate / (1.0 + jnp.exp(-gate)) * upper).astype(jnp.bfloat16)
    for copy in copies[chunks]:
        copy.wait()
    results = []
    for j, part in enumerate(parts):
        out[:, part] = jnp.dot(act, back[:, part], preferred_element_type=jnp.float32).astype(
            jnp.bfloat16
        )
        results.append(
            pltpu.make_async_copy(out.at[:, part], out_ref.at[:, part], sems.at[chunks * 5 + 2 + j])
        )
        results[-1].start()
    for copy in results:
        copy.wait()


def expert_pair(rows, gate_a, up_a, gate_b, up_b, down_a, down_b):
    count, width = rows.shape
    hidden = gate_a.shape[-1]
    chunks = 4
    anywhere = pl.BlockSpec(memory_space=pl.ANY)
    return pl.pallas_call(
        lambda *refs: expert_kernel(chunks, *refs),
        in_specs=[anywhere] * 7,
        out_specs=anywhere,
        out_shape=jax.ShapeDtypeStruct((count, width), jnp.bfloat16),
        scratch_shapes=[
            pltpu.VMEM((count, width), jnp.bfloat16),
            pltpu.VMEM((width, 4 * hidden), jnp.bfloat16),
            pltpu.VMEM((2 * hidden, width), jnp.bfloat16),
            pltpu.VMEM((count, width), jnp.bfloat16),
            pltpu.SemaphoreType.DMA((chunks * 6 + 2,)),
        ],
        compiler_params=pltpu.CompilerParams(vmem_limit_bytes=60 * 1024 * 1024),
        cost_estimate=pl.CostEstimate(
            flops=12 * count * width * hidden,
            bytes_accessed=4 * count * width + 12 * width * hidden,
            transcendentals=2 * count * hidden,
        ),
    )(rows, gate_a, up_a, gate_b, up_b, down_a, down_b)


def sum_over_cores(give, keep):
    n_y = lax.axis_size("y")
    got = lax.ppermute(give.astype(jnp.bfloat16), "core", SWAP)
    both = (keep + got.astype(jnp.float32)).astype(jnp.bfloat16)
    return both.reshape(n_y, both.shape[0] // n_y, -1)


def to_owners(blocks):
    return lax.all_to_all(blocks, "y", split_axis=0, concat_axis=0, tiled=True)


def add_terms(ref):
    total = ref[0].astype(jnp.float32)
    for i in range(1, ref.shape[0]):
        total += ref[i].astype(jnp.float32)
    return total


def stream_kernel(terms_ref, residual_ref, gain_ref, stream_ref, normed_ref):
    stream = residual_ref[...].astype(jnp.float32) + add_terms(terms_ref)
    mean_square = jnp.mean(stream * stream, axis=-1, keepdims=True)
    stream_ref[...] = stream
    normed_ref[...] = (stream * lax.rsqrt(mean_square + 1e-06) * gain_ref[...]).astype(
        jnp.bfloat16
    )


def finish_kernel(terms_ref, stream_ref, out_ref):
    out_ref[...] = (stream_ref[...] + add_terms(terms_ref)).astype(jnp.bfloat16)


def on_vmem(kernel, out_shape, *arguments):
    whole = pl.BlockSpec(memory_space=pltpu.VMEM)
    return pl.pallas_call(
        kernel,
        in_specs=[whole] * len(arguments),
        out_specs=jax.tree.map(lambda _: whole, out_shape),
        out_shape=out_shape,
        compiler_params=pltpu.CompilerParams(vmem_limit_bytes=4 * 1024 * 1024),
    )(*arguments)


def body(
    residual_in,
    queries,
    projected_key_value,
    query_gain,
    key_norm_gain,
    output_weight,
    norm_gain,
    gate_weight,
    up_weight,
    down_weight,
    expert_index,
    expert_slot,
    route_weight,
):
    rows = queries.shape[0]
    head_dim = query_gain.shape[0]
    local_heads = queries.shape[1] // head_dim
    n_x = lax.axis_size("xh") * lax.axis_size("xl")
    n_z = lax.axis_size("z")
    n_ctx = n_x * n_z
    n_exp = lax.axis_size("y") * lax.axis_size("core")
    core = lax.axis_index("core")
    ctx_index = lax.axis_index("z") * n_x + lax.axis_index("xh") * 2 + lax.axis_index("xl")
    exp_index = lax.axis_index("y") * 2 + core
    key_value_head = exp_index * local_heads // (QUERY_HEADS // KEY_VALUE_HEADS)
    place = jnp.stack([core, ctx_index, key_value_head]).astype(jnp.int32)
    table = jnp.asarray(tables(n_ctx * rows, head_dim))

    gate_other = lax.ppermute(gate_weight, "xl", SWAP)
    up_other = lax.ppermute(up_weight, "xl", SWAP)
    down_other = lax.ppermute(down_weight, "xl", SWAP)

    mine, query = prepare(
        place,
        projected_key_value,
        queries,
        key_norm_gain[None, :],
        query_gain[None, :],
        table,
        n_z,
    )
    mine = lax.all_to_all(mine, "z", split_axis=0, concat_axis=0, tiled=True)
    mine, gate_other = lax.optimization_barrier((mine, gate_other))
    mine = lax.all_gather(mine[None], ("xh", "xl"), axis=0, tiled=True)
    mine = mine.reshape(n_ctx * rows, head_dim)
    other = lax.ppermute(mine, "core", SWAP)
    attended = attend(place, query, mine, other, rows, n_x)
    give, keep = project(attended, output_weight)
    local = EXPERTS // n_exp
    pairs = SLICES // 2
    peers = local * pairs
    lanes = peers * CAP
    lane = jnp.arange(lanes, dtype=jnp.int32)
    lane_expert = lane // (pairs * CAP) + exp_index * local
    lane_slot = lane % CAP
    match = (expert_index[:, :, None] == lane_expert) & (expert_slot[:, :, None] == lane_slot)
    select = jnp.any(match, axis=1).astype(jnp.bfloat16)
    share = rows // n_exp
    own_residual = lax.dynamic_slice_in_dim(residual_in, exp_index * share, share, 0)
    both = sum_over_cores(give, keep)
    both, own_residual, select = lax.optimization_barrier((both, own_residual, select))
    width = own_residual.shape[-1]
    own_stream, own_normed = on_vmem(
        stream_kernel,
        [
            jax.ShapeDtypeStruct((share, width), jnp.float32),
            jax.ShapeDtypeStruct((share, width), jnp.bfloat16),
        ],
        to_owners(both),
        own_residual,
        norm_gain[None, :],
    )
    normed = lax.all_gather(own_normed, EXP, axis=0, tiled=True)
    normed, up_other = lax.optimization_barrier((normed, up_other))

    combine = jnp.sum(jnp.where(match, route_weight[:, :, None], 0.0), axis=1)
    combine = combine.reshape(n_exp // 2, 2, share, lanes)
    combine = jnp.concatenate(
        [lax.dynamic_index_in_dim(combine, i, 1, False) for i in (1 - core, core)], axis=0
    ).reshape(rows, lanes)
    combine_high = combine.astype(jnp.bfloat16)
    combine_low = (combine - combine_high.astype(jnp.float32)).astype(jnp.bfloat16)
    combine = jnp.concatenate([combine_high, combine_low], axis=0)

    outgoing = lax.dot_general(
        select, normed, (((0,), (0,)), ((), ())), preferred_element_type=jnp.float32
    ).astype(jnp.bfloat16)
    outgoing = outgoing.reshape(peers, CAP, width)
    arrived = lax.all_to_all(outgoing, ("z", "xh"), split_axis=0, concat_axis=0, tiled=True)
    pieces = expert_pair(
        arrived.reshape(lanes, width),
        gate_weight,
        up_weight,
        gate_other,
        up_other,
        down_weight,
        down_other,
    ).reshape(peers, CAP, width)
    returned = lax.all_to_all(pieces, ("z", "xh"), split_axis=0, concat_axis=0, tiled=True)
    returned = returned.reshape(lanes, width)
    mixture = jnp.dot(combine, returned, preferred_element_type=jnp.float32)
    mixture = mixture[:rows] + mixture[rows:]
    return on_vmem(
        finish_kernel,
        jax.ShapeDtypeStruct((share, width), jnp.bfloat16),
        to_owners(sum_over_cores(mixture[: rows // 2], mixture[rows // 2 :])),
        own_stream,
    )


def solution(mesh):
    shape = (12, 2, 2, 8, 2)
    fine = Mesh(np.asarray(mesh.devices).reshape(shape), CTX + EXP)
    in_specs = (
        P(CTX, None),
        P(CTX, EXP),
        P(None, CTX, None),
        P(),
        P(),
        P(EXP, None),
        P(),
        P(EXP + CTX, None, None),
        P(EXP + CTX, None, None),
        P(EXP + CTX, None, None),
        P(CTX, None),
        P(CTX, None),
        P(CTX, None),
    )
    out_specs = P(CTX + EXP, None)
    return jax.shard_map(body, mesh=fine, in_specs=in_specs, out_specs=out_specs, check_vma=False)
```
